256 devices in a mesh: fsdp: 16 (over z_lo, y), tp: 16 (over z_hi, x, core).
Axes of the slice: x: 4, y: 4, z: 8 (z_hi: 2, z_lo: 4; z = z_hi * 4 + z_lo), core: 2. Of those that a mesh axis runs over, the one named last changes fastest.
Arguments:
- output_gradient: bfloat16 [8192, 8192], P('fsdp'), may hold values from -6 to 6
- gate_pre: bfloat16 [8192, 14336], P('fsdp', 'tp'), may hold values from -6 to 6
- up_pre: bfloat16 [8192, 14336], P('fsdp', 'tp'), may hold values from -6 to 6
- down_weight: bfloat16 [14336, 8192], P('tp', 'fsdp'), may hold values from -0.046875 to 0.046875
- a_mean: float32 [8, 14336], P(None, 'tp'), may hold values from -0.75 to 0.75
- a_sigma: float32 [8, 14336], P(None, 'tp'), may hold values from 0.02 to 0.1
- a_noise: float32 [8, 14336], P(None, 'tp'), may hold values from -6 to 6
- second_factor: float32 [8, 8192], replicated, may hold values from -0.3125 to 0.3125
- in_signs: int32 [8192, 14336], P('fsdp', 'tp'), may hold values from -1 to 1, as said below
- out_signs: int32 [8192, 8], P('fsdp'), may hold values from -1 to 1, as said below
Outputs:
- d_gate: bfloat16 [8192, 14336], P('fsdp', 'tp')
- d_up: bfloat16 [8192, 14336], P('fsdp', 'tp')
- d_mean: float32 [8, 14336], P(None, 'tp')
- d_sigma: float32 [8, 14336], P(None, 'tp')
- second_factor_gradient: float32 [8, 8192], P(None, 'tp')
The draws below stay inside these ranges and needn't reach their ends.
Inputs may be any that keep to these rules, and one draw needn't show every extreme that they name: `in_signs`: every entry is -1 or +1. `out_signs`: every entry is -1 or +1.
All inputs are finite; a program needn't handle non-finite values.
Results may differ from the reference program's by a relative error of at most 0.0031.
Values may be sent and summed in bfloat16 or wider, within the bound.
A program may use at most 128 MiB of HBM per device.

```python
import math
import jax
import jax.numpy as jnp
from jax import lax

D = 8192
FF = 14336
RANK = 8
TOKENS = 8192


def draw_in_signs(key, part):
    return (2 * jax.random.randint(key, (TOKENS, FF), 0, 2) - 1).astype(jnp.int32)


def draw_out_signs(key, part):
    return (2 * jax.random.randint(key, (TOKENS, RANK), 0, 2) - 1).astype(jnp.int32)


def block_scale(key, shape, pieces, low, top_value):
    gain = 1.0
    for axis_at, parts in pieces:
        draws = jax.random.uniform(jax.random.fold_in(jax.random.fold_in(key, 6), axis_at), (parts,), jnp.float32, low / len(pieces), top_value / len(pieces))
        gain = gain * jnp.repeat(jnp.exp(draws), shape[axis_at] // parts).reshape((-1,) + (1,) * (len(shape) - 1 - axis_at))
    return gain


def centred(rng, extent, scale, limit, split=(), kind=jnp.bfloat16):
    array = scale * jax.random.normal(rng, extent, jnp.float32)
    if split:
        array = array * block_scale(rng, extent, split, -0.22, 0.18)
    return jnp.clip(array, -limit, limit).astype(kind)


def setup_inputs(seed: int = 0) -> dict:
    arg_keys = jax.random.split(jax.random.key(seed), 11)
    output_gradient = centred(arg_keys[0], (TOKENS, D), 1.0, 6.0, ((0, 16),))
    gate_pre = centred(arg_keys[1], (TOKENS, FF), 1.0, 6.0, ((0, 16), (1, 16)))
    up_pre = centred(arg_keys[2], (TOKENS, FF), 1.0, 6.0, ((0, 16), (1, 16)))
    down_weight = centred(arg_keys[3], (FF, D), FF ** -0.5, 0.046875, ((0, 16), (1, 16)))
    a_mean = centred(arg_keys[4], (RANK, FF), 0.05, 0.75, ((1, 16),), jnp.float32)
    a_sigma = jnp.clip(jnp.exp(math.log(0.1) - 1.609438 * jax.random.uniform(arg_keys[5], (RANK, FF), jnp.float32) ** block_scale(arg_keys[5], (RANK, FF), ((1, 16),), -0.2, 0.2)), 0.02, 0.1)
    a_noise = centred(arg_keys[6], (RANK, FF), 1.0, 6.0, ((1, 16),), jnp.float32)
    second_factor = centred(arg_keys[7], (RANK, D), 0.022, 0.3125, (), jnp.float32)
    in_signs = draw_in_signs(jax.random.fold_in(arg_keys[10], 71), 0)
    out_signs = draw_out_signs(jax.random.fold_in(arg_keys[10], 71), 0)
    return {"output_gradient": output_gradient, "gate_pre": gate_pre, "up_pre": up_pre, "down_weight": down_weight, "a_mean": a_mean, "a_sigma": a_sigma, "a_noise": a_noise, "second_factor": second_factor, "in_signs": in_signs, "out_signs": out_signs}


adapter_scale = 2.0

def reference(output_gradient, gate_pre, up_pre, down_weight, a_mean, a_sigma, a_noise, second_factor, in_signs, out_signs):
    highest_precision = lax.Precision.HIGHEST
    gate_wide = gate_pre.astype(jnp.float32)
    up_wide = up_pre.astype(jnp.float32)
    sigmoid_gate = jax.nn.sigmoid(gate_wide)
    hidden = (gate_wide * sigmoid_gate * up_wide).astype(jnp.bfloat16)
    spread = a_sigma * a_noise
    sign_in = in_signs.astype(jnp.float32)
    sign_out = out_signs.astype(jnp.float32)
    flipped = hidden * sign_in
    rank_values = jnp.dot(hidden, a_mean.T, precision=highest_precision, preferred_element_type=jnp.float32) + sign_out * jnp.dot(flipped, spread.T, precision=highest_precision, preferred_element_type=jnp.float32)
    rank_gradient = adapter_scale * jnp.dot(output_gradient, second_factor.T, precision=highest_precision, preferred_element_type=jnp.float32)
    base_grad = lax.dot_general(output_gradient, down_weight, (((1,), (1,)), ((), ())), preferred_element_type=jnp.float32)
    signed_grad = rank_gradient * sign_out
    hidden_grad = base_grad + jnp.dot(rank_gradient, a_mean, precision=highest_precision, preferred_element_type=jnp.float32) + sign_in * jnp.dot(signed_grad, spread, precision=highest_precision, preferred_element_type=jnp.float32)
    d_gate = (hidden_grad * up_wide * sigmoid_gate * (1.0 + gate_wide * (1.0 - sigmoid_gate))).astype(jnp.bfloat16)
    d_up = (hidden_grad * gate_wide * sigmoid_gate).astype(jnp.bfloat16)
    normalizing_count = 1.0 / math.sqrt(TOKENS)
    d_mean = normalizing_count * jnp.dot(rank_gradient.T, hidden, precision=highest_precision, preferred_element_type=jnp.float32)
    d_sigma = normalizing_count * a_noise * jnp.dot(signed_grad.T, flipped, precision=highest_precision, preferred_element_type=jnp.float32)
    second_factor_gradient = normalizing_count * adapter_scale * jnp.dot(rank_values.T, output_gradient, precision=highest_precision, preferred_element_type=jnp.float32)
    return (d_gate, d_up, d_mean, d_sigma, second_factor_gradient)
```

```python
import math

import jax
import jax.numpy as jnp
from jax import lax
from jax.experimental import pallas as pl
from jax.experimental.pallas import tpu as pltpu
from jax.sharding import PartitionSpec as P

MESH = pl.DeviceIdType.MESH
F32 = jnp.float32
BF16 = jnp.bfloat16
adapter_scale = 2.0

TOK = 512
WID = 512
HID = 896
CH = 128
NCH = HID // CH
HALF = 2048
RED = 2 * HID + WID


def nt(left, right):
    return lax.dot_general(left, right, (((1,), (1,)), ((), ())), preferred_element_type=F32)


def nn(left, right):
    return lax.dot_general(left, right, (((1,), (0,)), ((), ())), preferred_element_type=F32)


def thirds(value):
    first = value.astype(BF16).astype(F32)
    rest = value - first
    second = rest.astype(BF16).astype(F32)
    third = (rest - second).astype(BF16).astype(F32)
    return first, second, third


def kernel(
    og,
    gate,
    up,
    dw,
    a_mean,
    a_sigma,
    a_noise,
    factor,
    in_signs,
    out_signs,
    d_gate,
    d_up,
    d_mean,
    d_sigma,
    d_factor,
    DW,
    OGO,
    OGX,
    OGP,
    OGC,
    G,
    U,
    IS,
    H,
    HS,
    CA,
    CB,
    OWN,
    PACC,
    RSS,
    RSR,
    SF,
    LT,
    R1,
    R2,
    SO,
    RVS,
    RVR,
    RY,
    RZ,
    local_sem,
    send_dw,
    send_og,
    send_rs,
    send_rv,
    send_ry,
    send_rz,
    rz,
    ra,
    rb,
    rc,
    rp,
    rr,
    rv,
    ry,
    rzz,
):
    fi = lax.axis_index("fsdp")
    tj = lax.axis_index("tp")
    y, z = lax.rem(fi, 4), lax.div(fi, 4)
    c, x, zh = lax.rem(tj, 2), lax.rem(lax.div(tj, 2), 4), lax.div(tj, 8)
    par, h0 = lax.rem(z, 2), lax.div(z, 2)
    h1 = 1 - h0

    def at(px=x, py=y, pz=z, pzh=zh, pc=c):
        return (pz * 4 + py, (pzh * 4 + px) * 2 + pc)

    def ring(value, step):
        return lax.rem(value + step, 4)

    right, left = at(py=ring(y, 1)), at(py=ring(y, 3))
    pair = at(pz=z + 1 - 2 * par)
    across = at(pz=ring(z, 2))
    sibling = at(pc=1 - c)
    other_hi = at(pzh=1 - zh)
    ys = [at(py=ring(y, d)) for d in (1, 2, 3)]
    zs = [at(pz=ring(z, d)) for d in (1, 2, 3)]
    xs = [at(px=ring(x, d)) for d in (1, 2, 3)]

    barrier = pltpu.get_barrier_semaphore()
    partners = ys + zs + xs + [sibling, other_hi]
    for partner in partners:
        pl.semaphore_signal(barrier, inc=1, device_id=partner, device_id_type=MESH)

    own = h0 * 4 + y
    mirror = h1 * 4 + y

    local = [
        pltpu.make_async_copy(dw, DW.at[own], local_sem.at[0]),
        pltpu.make_async_copy(gate, G, local_sem.at[1]),
        pltpu.make_async_copy(up, U, local_sem.at[2]),
        pltpu.make_async_copy(in_signs, IS, local_sem.at[3]),
    ]
    for h in range(2):
        mine = pl.ds(pl.multiple_of((2 * h + par) * HALF, HALF), HALF)
        rest = pl.ds(pl.multiple_of((2 * h + 1 - par) * HALF, HALF), HALF)
        local.append(pltpu.make_async_copy(og.at[:, mine], OGO.at[h], local_sem.at[4 + 2 * h]))
        local.append(pltpu.make_async_copy(og.at[:, rest], OGX.at[h], local_sem.at[5 + 2 * h]))
    out_cols = pl.ds(pl.multiple_of(tj * WID, WID), WID)
    local.append(pltpu.make_async_copy(og.at[:, out_cols], OGC, local_sem.at[8]))
    for copy in local:
        copy.start()

    pl.semaphore_wait(barrier, len(partners))

    def send(src, dst, send_sem, recv_sem, device):
        pltpu.make_async_remote_copy(
            src_ref=src,
            dst_ref=dst,
            send_sem=send_sem,
            recv_sem=recv_sem,
            device_id=device,
            device_id_type=MESH,
        ).start()

    def landed(ref, sem):
        pltpu.make_async_copy(ref, ref, sem).wait()

    def piece(q, h):
        return OGP.at[h, pl.ds(pl.multiple_of(q * 64, 64), 64)]

    q_own = x * 2 + c

    def step_p(h):
        rows = pl.ds(pl.multiple_of(q_own * 64, 64), 64)
        cols = pl.ds(pl.multiple_of((2 * h + 1 - par) * HALF, HALF), HALF)
        send(og.at[rows, cols], piece(q_own, h), send_og, rp.at[q_own, h], pair)

    def step_x(h):
        landed(piece(q_own, h), rp.at[q_own, h])
        for device in xs + [sibling]:
            send(piece(q_own, h), piece(q_own, h), send_og, rp.at[q_own, h], device)

    def step_y(h):
        for d in (1, 3, 2):
            q = ring(x, d) * 2 + c
            landed(piece(q, h), rp.at[q, h])
            send(piece(q, h), piece(q, h), send_og, rp.at[q, h], sibling)

    def step_w(h):
        for px in range(4):
            q = px * 2 + 1 - c
            landed(piece(q, h), rp.at[q, h])

    def rows_of(slot, k, part=None):
        if part is None:
            return DW.at[slot, pl.ds(k * CH, CH)]
        return DW.at[slot, pl.ds(k * CH + part * (CH // 2), CH // 2)]

    def step_z(k):
        send(rows_of(own, k), rows_of(own, k), send_dw, rz.at[k], across)

    def step_a(k):
        send(rows_of(own, k), rows_of(own, k), send_dw, ra.at[0, k], right)
        send(rows_of(own, k), rows_of(own, k), send_dw, ra.at[1, k], left)

    def step_b(k):
        landed(rows_of(mirror, k), rz.at[k])
        send(rows_of(mirror, k), rows_of(mirror, k), send_dw, rb.at[0, k], right)
        send(rows_of(mirror, k), rows_of(mirror, k), send_dw, rb.at[1, k], left)

    def relay(sems, h, group, k):
        slot = h * 4 + ring(y, 3)
        landed(rows_of(slot, k), sems.at[0, k])
        send(rows_of(slot, k, 0), rows_of(slot, k, 0), send_dw, rc.at[0, group, k], right)
        slot = h * 4 + ring(y, 1)
        landed(rows_of(slot, k), sems.at[1, k])
        send(rows_of(slot, k, 1), rows_of(slot, k, 1), send_dw, rc.at[1, group, k], left)

    def step_c(k):
        relay(ra, h0, 0, k)

    def step_d(k):
        relay(rb, h1, 1, k)

    def step_e(k):
        for group, h in ((0, h0), (1, h1)):
            for part in range(2):
                landed(rows_of(h * 4 + ring(y, 2), k, part), rc.at[part, group, k])

    def matmul(k, count):
        rows = pl.ds(k * CH, count * CH)
        cols = slice(k * CH, (k + count) * CH)
        wide = slice(0, count * CH)
        PACC[:, wide] = jnp.zeros((TOK, count * CH), F32)

        def part(src, acc, acc_cols):
            def body(s, carry):
                kcols = pl.ds(pl.multiple_of(lax.rem(s, 4) * WID, WID), WID)
                acc[:, acc_cols] += nt(src[lax.div(s, 4), :, kcols], DW[s, rows, :])
                return carry

            lax.fori_loop(0, 8, body, 0)

        part(OGP, PACC, wide)
        for n in range(count):
            RSS[k + n] = PACC[:, n * CH : (n + 1) * CH].astype(BF16)
            send(RSS.at[k + n], RSR.at[k + n], send_rs, rr.at[k + n], pair)
        part(OGO, OWN, cols)

    def finish(k):
        cols = slice(k * CH, (k + 1) * CH)
        landed(RSR.at[k], rr.at[k])
        hidden_grad = OWN[:, cols] + RSR[k].astype(F32)
        d_gate[:, cols] = (hidden_grad * CA[:, cols]).astype(BF16)
        d_up[:, cols] = (hidden_grad * CB[:, cols]).astype(BF16)

    step_p(0)
    step_p(1)
    local[0].wait()
    for k in range(NCH):
        step_z(k)
        if k < 3:
            step_a(k)

    for n in (1, 2, 3):
        local[n].wait()

    def pre(k, carry):
        cols = pl.ds(pl.multiple_of(k * CH, CH), CH)
        g = G[:, cols].astype(F32)
        u = U[:, cols].astype(F32)
        s = jax.nn.sigmoid(g)
        hidden = (g * s * u).astype(BF16)
        H[:, cols] = hidden
        HS[:, cols] = (hidden.astype(F32) * IS[:, cols].astype(F32)).astype(BF16)
        CA[:, cols] = u * s * (1.0 + g * (1.0 - s))
        CB[:, cols] = g * s
        return carry

    lax.fori_loop(0, NCH, pre, 0)

    spread = a_sigma[...] * a_noise[...]
    am = thirds(a_mean[...])
    sp = thirds(spread)
    gap = jnp.zeros((8, HID), F32)
    R1[...] = jnp.concatenate([am[0], am[1], am[2]] + [gap] * 13, axis=0).astype(BF16)
    R2[...] = jnp.concatenate([gap] * 4 + [sp[0], sp[1], sp[2]] + [gap] * 9, axis=0).astype(BF16)
    eye = (
        lax.broadcasted_iota(jnp.int32, (8, 8), 0) == lax.broadcasted_iota(jnp.int32, (8, 8), 1)
    ).astype(F32)
    SO[...] = nt(eye, out_signs[...].astype(F32))
    both = (nt(H[...], R1[...]) + nt(HS[...], R2[...])).T
    RVS[0] = (both[0:8] + both[8:16] + both[16:24]) + SO[...] * (
        both[32:40] + both[40:48] + both[48:56]
    )
    send(RVS.at[0], RVR.at[0], send_rv.at[0], rv.at[0], sibling)

    step_c(0)
    step_a(3)
    step_b(0)
    step_x(0)

    sf = thirds(factor[...])
    SF[...] = jnp.concatenate(
        [sf[0], sf[1], sf[2]] + [jnp.zeros((8, 4 * HALF), F32)] * 13, axis=0
    ).astype(BF16)
    LTF = None
    for n in range(4, 9):
        local[n].wait()
    for h in range(2):
        mine = pl.ds(pl.multiple_of((2 * h + par) * HALF, HALF), HALF)
        rest = pl.ds(pl.multiple_of((2 * h + 1 - par) * HALF, HALF), HALF)
        term = nt(OGO[h], SF[:, mine]) + nt(OGX[h], SF[:, rest])
        LTF = term if LTF is None else LTF + term
    turned = LTF.T
    rank_grad = adapter_scale * (turned[0:8] + turned[8:16] + turned[16:24])
    signed = rank_grad * SO[...]
    rg = thirds(rank_grad)
    sg = thirds(signed)

    step_c(1)
    step_a(4)
    step_b(1)
    step_d(0)
    step_x(1)

    landed(RVR.at[0], rv.at[0])
    RVS[1] = RVS[0] + RVR[0]
    for d in (1, 2, 3):
        send(RVS.at[1], RVR.at[d], send_rv.at[d], rv.at[d], xs[d - 1])

    blank = jnp.zeros((8, TOK), F32)
    LT[...] = (
        jnp.concatenate(
            [rg[0], rg[0], rg[1], rg[1], rg[0], rg[2], blank, blank]
            + [sg[0], sg[0], sg[1], sg[1], sg[0], sg[2], blank, blank],
            axis=0,
        )
        .T.astype(BF16)
    )
    mean3 = nn(jnp.concatenate(list(rg) + [blank], axis=0).astype(BF16), H[...])
    sigma3 = nn(jnp.concatenate(list(sg) + [blank], axis=0).astype(BF16), HS[...])
    RY[y, :, 0:HID] = mean3[0:8] + mean3[8:16] + mean3[16:24]
    RY[y, :, HID : 2 * HID] = sigma3[0:8] + sigma3[8:16] + sigma3[16:24]
    R1[...] = jnp.concatenate(
        [am[0], am[1], am[0], am[1], am[2], am[0]] + [gap] * 10, axis=0
    ).astype(BF16)
    R2[...] = jnp.concatenate(
        [gap] * 8 + [sp[0], sp[1], sp[0], sp[1], sp[2], sp[0]] + [gap] * 2, axis=0
    ).astype(BF16)

    def rank_terms(k, carry):
        cols = pl.ds(pl.multiple_of(k * CH, CH), CH)
        OWN[:, cols] = nn(LT[...], R1[:, cols]) + IS[:, cols].astype(F32) * nn(LT[...], R2[:, cols])
        return carry

    lax.fori_loop(0, NCH, rank_terms, 0)

    step_y(0)
    step_c(2)
    step_a(5)
    step_b(2)
    step_d(1)

    for d in (1, 2, 3):
        landed(RVR.at[d], rv.at[d])
    RVS[2] = RVS[1] + RVR[1] + RVR[2] + RVR[3]
    send(RVS.at[2], RVR.at[4], send_rv.at[4], rv.at[4], other_hi)

    step_y(1)
    step_w(0)
    step_c(3)
    step_a(6)
    step_b(3)
    step_d(2)
    step_w(1)

    landed(RVR.at[4], rv.at[4])
    ranks = thirds(RVS[2] + RVR[4])
    factor3 = nn(jnp.concatenate(list(ranks) + [blank], axis=0).astype(BF16), OGC[...])
    RY[y, :, 2 * HID :] = factor3[0:8] + factor3[8:16] + factor3[16:24]
    for d in (1, 2, 3):
        send(RY.at[y], RY.at[y], send_ry.at[d - 1], ry.at[d - 1], ys[d - 1])

    step_e(0)
    step_e(1)
    matmul(0, 2)

    step_c(4)
    step_b(4)
    step_d(3)

    for d in (1, 2, 3):
        landed(RY.at[ring(y, 4 - d)], ry.at[d - 1])
    RZ[z] = ((RY[0] + RY[1]) + RY[2]) + RY[3]
    for d in (1, 2, 3):
        send(RZ.at[z], RZ.at[z], send_rz.at[d - 1], rzz.at[d - 1], zs[d - 1])

    step_e(2)
    step_e(3)
    matmul(2, 2)
    step_c(5)
    step_b(5)
    step_d(4)
    finish(0)
    finish(1)

    for d in (1, 2, 3):
        landed(RZ.at[ring(z, 4 - d)], rzz.at[d - 1])
    total = ((RZ[0] + RZ[1]) + RZ[2]) + RZ[3]
    count = 1.0 / math.sqrt(TOK * 16)
    d_mean[...] = count * total[:, 0:HID]
    d_sigma[...] = count * a_noise[...] * total[:, HID : 2 * HID]
    d_factor[...] = (count * adapter_scale) * total[:, 2 * HID :]

    step_c(6)
    step_b(6)
    step_d(5)
    step_e(4)
    step_e(5)
    matmul(4, 2)
    step_d(6)
    finish(2)
    finish(3)
    step_e(6)
    matmul(6, 1)
    finish(4)
    finish(5)
    finish(6)

    landed(DW.at[pl.ds(0, 7)], send_dw)
    landed(OGP, send_og)
    landed(RSS, send_rs)
    landed(RVS.at[0], send_rv.at[0])
    for d in (1, 2, 3):
        landed(RVS.at[1], send_rv.at[d])
        landed(RY.at[y], send_ry.at[d - 1])
        landed(RZ.at[z], send_rz.at[d - 1])
    landed(RVS.at[2], send_rv.at[4])


def local(*args):
    vmem = pl.BlockSpec(memory_space=pltpu.VMEM)
    anywhere = pl.BlockSpec(memory_space=pl.ANY)
    dma = pltpu.SemaphoreType.DMA
    scratch = [
        pltpu.VMEM((8, HID, WID), BF16),
        pltpu.VMEM((2, TOK, HALF), BF16),
        pltpu.VMEM((2, TOK, HALF), BF16),
        pltpu.VMEM((2, TOK, HALF), BF16),
        pltpu.VMEM((TOK, WID), BF16),
        pltpu.VMEM((TOK, HID), BF16),
        pltpu.VMEM((TOK, HID), BF16),
        pltpu.VMEM((TOK, HID), jnp.int32),
        pltpu.VMEM((TOK, HID), BF16),
        pltpu.VMEM((TOK, HID), BF16),
        pltpu.VMEM((TOK, HID), F32),
        pltpu.VMEM((TOK, HID), F32),
        pltpu.VMEM((TOK, HID), F32),
        pltpu.VMEM((TOK, 2 * CH), F32),
        pltpu.VMEM((NCH, TOK, CH), BF16),
        pltpu.VMEM((NCH, TOK, CH), BF16),
        pltpu.VMEM((128, 4 * HALF), BF16),
        pltpu.VMEM((TOK, 128), BF16),
        pltpu.VMEM((128, HID), BF16),
        pltpu.VMEM((128, HID), BF16),
        pltpu.VMEM((8, TOK), F32),
        pltpu.VMEM((3, 8, TOK), F32),
        pltpu.VMEM((5, 8, TOK), F32),
        pltpu.VMEM((4, 8, RED), F32),
        pltpu.VMEM((4, 8, RED), F32),
        dma((9,)),
        dma(()),
        dma(()),
        dma(()),
        dma((5,)),
        dma((3,)),
        dma((3,)),
        dma((NCH,)),
        dma((2, NCH)),
        dma((2, NCH)),
        dma((2, 2, NCH)),
        dma((8, 2)),
        dma((NCH,)),
        dma((5,)),
        dma((3,)),
        dma((3,)),
    ]
    return pl.pallas_call(
        kernel,
        out_shape=(
            jax.ShapeDtypeStruct((TOK, HID), BF16),
            jax.ShapeDtypeStruct((TOK, HID), BF16),
            jax.ShapeDtypeStruct((8, HID), F32),
            jax.ShapeDtypeStruct((8, HID), F32),
            jax.ShapeDtypeStruct((8, WID), F32),
        ),
        in_specs=[anywhere] * 4 + [vmem] * 4 + [anywhere, vmem],
        out_specs=(vmem,) * 5,
        scratch_shapes=scratch,
        compiler_params=pltpu.CompilerParams(
            collective_id=0, has_side_effects=True, vmem_limit_bytes=58 * 2**20
        ),
        name="ffn_backward",
    )(*args)


def solution(mesh):
    placed = (
        P("fsdp", None),
        P("fsdp", "tp"),
        P("fsdp", "tp"),
        P("tp", "fsdp"),
        P(None, "tp"),
        P(None, "tp"),
        P(None, "tp"),
        P(),
        P("fsdp", "tp"),
        P("fsdp", None),
    )
    return jax.shard_map(
        local,
        mesh=mesh,
        in_specs=placed,
        out_specs=(P("fsdp", "tp"), P("fsdp", "tp"), P(None, "tp"), P(None, "tp"), P(None, "tp")),
        check_vma=False,
    )
```

```python
import math

import jax
import jax.numpy as jnp
from jax import lax
from jax.experimental import pallas as pl
from jax.experimental.pallas import tpu as pltpu
from jax.sharding import PartitionSpec as P

MESH = pl.DeviceIdType.MESH
F32 = jnp.float32
BF16 = jnp.bfloat16
adapter_scale = 2.0

TOK = 512
WID = 512
HID = 896
CH = 128
NCH = HID // CH
HALF = 2048
RED = 2 * HID + WID


def nt(left, right):
    return lax.dot_general(left, right, (((1,), (1,)), ((), ())), preferred_element_type=F32)


def nn(left, right):
    return lax.dot_general(left, right, (((1,), (0,)), ((), ())), preferred_element_type=F32)


def thirds(value):
    first = value.astype(BF16).astype(F32)
    rest = value - first
    second = rest.astype(BF16).astype(F32)
    third = (rest - second).astype(BF16).astype(F32)
    return first, second, third


def kernel(
    og,
    gate,
    up,
    dw,
    a_mean_in,
    a_sigma_in,
    a_noise_in,
    factor_in,
    in_signs,
    out_signs_in,
    d_gate,
    d_up,
    d_mean,
    d_sigma,
    d_factor,
    DW,
    OGO,
    OGX,
    OGP,
    OGC,
    G,
    U,
    IS,
    H,
    HS,
    CA,
    CB,
    OWN,
    PACC,
    RSS,
    RSR,
    SF,
    LT,
    R1,
    R2,
    RVS,
    RVR,
    RY,
    RZ,
    a_mean,
    a_sigma,
    a_noise,
    factor,
    out_signs,
    OM,
    OS,
    OF,
    local_sem,
    out_sem,
    send_dw,
    send_og,
    send_rs,
    send_rv,
    send_ry,
    send_rz,
    rz,
    ra,
    rb,
    rc,
    rp,
    rr,
    rv,
    ry,
    rzz,
):
    fi = lax.axis_index("fsdp")
    tj = lax.axis_index("tp")
    y, z = lax.rem(fi, 4), lax.div(fi, 4)
    c, x, zh = lax.rem(tj, 2), lax.rem(lax.div(tj, 2), 4), lax.div(tj, 8)
    par, h0 = lax.rem(z, 2), lax.div(z, 2)
    h1 = 1 - h0

    def at(px=x, py=y, pz=z, pzh=zh, pc=c):
        return (pz * 4 + py, (pzh * 4 + px) * 2 + pc)

    def ring(value, step):
        return lax.rem(value + step, 4)

    right, left = at(py=ring(y, 1)), at(py=ring(y, 3))
    pair = at(pz=z + 1 - 2 * par)
    across = at(pz=ring(z, 2))
    sibling = at(pc=1 - c)
    other_hi = at(pzh=1 - zh)
    ys = [at(py=ring(y, d)) for d in (1, 2, 3)]
    zs = [at(pz=ring(z, d)) for d in (1, 2, 3)]
    xs = [at(px=ring(x, d)) for d in (1, 2, 3)]

    barrier = pltpu.get_barrier_semaphore()
    partners = ys + zs + xs + [sibling, other_hi]
    for partner in partners:
        pl.semaphore_signal(barrier, inc=1, device_id=partner, device_id_type=MESH)

    own = h0 * 4 + y
    mirror = h1 * 4 + y

    local = [
        pltpu.make_async_copy(dw, DW.at[own], local_sem.at[0]),
        pltpu.make_async_copy(gate, G, local_sem.at[1]),
        pltpu.make_async_copy(up, U, local_sem.at[2]),
        pltpu.make_async_copy(in_signs, IS, local_sem.at[3]),
        pltpu.make_async_copy(a_mean_in, a_mean, local_sem.at[4]),
        pltpu.make_async_copy(a_sigma_in, a_sigma, local_sem.at[5]),
        pltpu.make_async_copy(a_noise_in, a_noise, local_sem.at[6]),
        pltpu.make_async_copy(out_signs_in, out_signs, local_sem.at[7]),
        pltpu.make_async_copy(factor_in, factor, local_sem.at[8]),
    ]
    early = len(local)
    for h in range(2):
        mine = pl.ds(pl.multiple_of((2 * h + par) * HALF, HALF), HALF)
        rest = pl.ds(pl.multiple_of((2 * h + 1 - par) * HALF, HALF), HALF)
        local.append(pltpu.make_async_copy(og.at[:, mine], OGO.at[h], local_sem.at[9 + 2 * h]))
        local.append(pltpu.make_async_copy(og.at[:, rest], OGX.at[h], local_sem.at[10 + 2 * h]))
    out_cols = pl.ds(pl.multiple_of(tj * WID, WID), WID)
    local.append(pltpu.make_async_copy(og.at[:, out_cols], OGC, local_sem.at[13]))
    for copy in local[1:early]:
        copy.start()

    pl.semaphore_wait(barrier, len(partners))

    def send(src, dst, send_sem, recv_sem, device):
        pltpu.make_async_remote_copy(
            src_ref=src,
            dst_ref=dst,
            send_sem=send_sem,
            recv_sem=recv_sem,
            device_id=device,
            device_id_type=MESH,
        ).start()

    def landed(ref, sem):
        pltpu.make_async_copy(ref, ref, sem).wait()

    def piece(q, h):
        return OGP.at[h, pl.ds(pl.multiple_of(q * 64, 64), 64)]

    q_own = x * 2 + c

    def step_p(h):
        rows = pl.ds(pl.multiple_of(q_own * 64, 64), 64)
        cols = pl.ds(pl.multiple_of((2 * h + 1 - par) * HALF, HALF), HALF)
        send(og.at[rows, cols], piece(q_own, h), send_og, rp.at[q_own, h], pair)

    def step_x(h):
        landed(piece(q_own, h), rp.at[q_own, h])
        for device in xs + [sibling]:
            send(piece(q_own, h), piece(q_own, h), send_og, rp.at[q_own, h], device)

    def step_y(h):
        for d in (1, 3, 2):
            q = ring(x, d) * 2 + c
            landed(piece(q, h), rp.at[q, h])
            send(piece(q, h), piece(q, h), send_og, rp.at[q, h], sibling)

    def step_w(h):
        for px in range(4):
            q = px * 2 + 1 - c
            landed(piece(q, h), rp.at[q, h])

    def rows_of(slot, k, part=None):
        if part is None:
            return DW.at[slot, pl.ds(k * CH, CH)]
        return DW.at[slot, pl.ds(k * CH + part * (CH // 2), CH // 2)]

    def step_z(k):
        send(dw.at[pl.ds(k * CH, CH)], rows_of(own, k), send_dw, rz.at[k], across)

    def step_a(k):
        send(dw.at[pl.ds(k * CH, CH)], rows_of(own, k), send_dw, ra.at[0, k], right)
        send(dw.at[pl.ds(k * CH, CH)], rows_of(own, k), send_dw, ra.at[1, k], left)

    def step_b(k):
        landed(rows_of(mirror, k), rz.at[k])
        send(rows_of(mirror, k), rows_of(mirror, k), send_dw, rb.at[0, k], right)
        send(rows_of(mirror, k), rows_of(mirror, k), send_dw, rb.at[1, k], left)

    def relay(sems, h, group, k):
        slot = h * 4 + ring(y, 3)
        landed(rows_of(slot, k), sems.at[0, k])
        send(rows_of(slot, k, 0), rows_of(slot, k, 0), send_dw, rc.at[0, group, k], right)
        slot = h * 4 + ring(y, 1)
        landed(rows_of(slot, k), sems.at[1, k])
        send(rows_of(slot, k, 1), rows_of(slot, k, 1), send_dw, rc.at[1, group, k], left)

    def step_c(k):
        relay(ra, h0, 0, k)

    def step_d(k):
        relay(rb, h1, 1, k)

    def step_e(k):
        for group, h in ((0, h0), (1, h1)):
            for part in range(2):
                landed(rows_of(h * 4 + ring(y, 2), k, part), rc.at[part, group, k])

    def part(src, acc, acc_cols, rows, low, high):
        def body(m, carry):
            py = ring(y, m + 3)
            kcols = pl.ds(pl.multiple_of(py * WID, WID), WID)
            acc[:, acc_cols] += nt(src[0, :, kcols], DW[py, rows, :]) + nt(src[1, :, kcols], DW[4 + py, rows, :])
            return carry

        lax.fori_loop(low // 2, high // 2, body, 0)

    def to_pair(k, n):
        RSS[k] = PACC[:, n * CH : (n + 1) * CH].astype(BF16)
        send(RSS.at[k], RSR.at[k], send_rs, rr.at[k], pair)

    def to_partner(k, count):
        wide = slice(0, count * CH)
        PACC[:, wide] = jnp.zeros((TOK, count * CH), F32)
        part(OGP, PACC, wide, pl.ds(k * CH, count * CH), 0, 8)
        for n in range(count):
            to_pair(k + n, n)

    def to_self(k, count):
        part(OGO, OWN, slice(k * CH, (k + count) * CH), pl.ds(k * CH, count * CH), 0, 8)

    out_copies = []

    def put(src, dst):
        copy = pltpu.make_async_copy(src, dst, out_sem.at[len(out_copies)])
        copy.start()
        out_copies.append(copy)

    def finish(k):
        cols = slice(k * CH, (k + 1) * CH)
        landed(RSR.at[k], rr.at[k])
        hidden_grad = OWN[:, cols] + RSR[k].astype(F32)
        G[:, cols] = (hidden_grad * CA[:, cols]).astype(BF16)
        U[:, cols] = (hidden_grad * CB[:, cols]).astype(BF16)
        put(G.at[:, pl.ds(k * CH, CH)], d_gate.at[:, pl.ds(k * CH, CH)])
        put(U.at[:, pl.ds(k * CH, CH)], d_up.at[:, pl.ds(k * CH, CH)])

    step_p(0)
    step_p(1)
    for k in range(NCH):
        step_a(k)
    for k in range(NCH):
        step_z(k)
    local[0].start()
    for copy in local[early:]:
        copy.start()

    for n in (1, 2, 3):
        local[n].wait()

    def pre(k, carry):
        cols = pl.ds(pl.multiple_of(k * CH, CH), CH)
        g = G[:, cols].astype(F32)
        u = U[:, cols].astype(F32)
        s = jax.nn.sigmoid(g)
        hidden = (g * s * u).astype(BF16)
        H[:, cols] = hidden
        HS[:, cols] = (hidden.astype(F32) * IS[:, cols].astype(F32)).astype(BF16)
        CA[:, cols] = u * s * (1.0 + g * (1.0 - s))
        CB[:, cols] = g * s
        return carry

    lax.fori_loop(0, NCH, pre, 0)

    for n in range(4, early):
        local[n].wait()
    spread = a_sigma[...] * a_noise[...]
    am = thirds(a_mean[...])
    sp = thirds(spread)
    gap = jnp.zeros((8, HID), F32)
    R1[...] = jnp.concatenate([am[0], am[1], am[2]] + [gap] * 13, axis=0).astype(BF16)
    R2[...] = jnp.concatenate([gap] * 4 + [sp[0], sp[1], sp[2]] + [gap] * 9, axis=0).astype(BF16)
    sign_out = out_signs[...].astype(F32)
    both = (nt(H[...], R1[...]) + nt(HS[...], R2[...])).T
    RVS[0] = (both[0:8] + both[8:16] + both[16:24]) + sign_out * (
        both[32:40] + both[40:48] + both[48:56]
    )
    send(RVS.at[0], RVR.at[0], send_rv.at[0], rv.at[0], sibling)

    step_x(0)
    step_c(0)
    sf = thirds(factor[...])
    SF[...] = jnp.concatenate(
        [sf[0], sf[1], sf[2]] + [jnp.zeros((8, 4 * HALF), F32)] * 13, axis=0
    ).astype(BF16)
    for n in range(early, len(local)):
        local[n].wait()
    local[0].wait()
    LTF = None
    for h in range(2):
        mine = pl.ds(pl.multiple_of((2 * h + par) * HALF, HALF), HALF)
        rest = pl.ds(pl.multiple_of((2 * h + 1 - par) * HALF, HALF), HALF)
        term = nt(OGO[h], SF[:, mine]) + nt(OGX[h], SF[:, rest])
        LTF = term if LTF is None else LTF + term
    turned = LTF.T
    rank_grad = adapter_scale * (turned[0:8] + turned[8:16] + turned[16:24])
    signed = rank_grad * sign_out
    rg = thirds(rank_grad)
    sg = thirds(signed)

    step_x(1)
    step_b(0)
    step_c(1)
    step_c(2)
    landed(RVR.at[0], rv.at[0])
    RVS[1] = RVS[0] + RVR[0]
    for d in (1, 2, 3):
        send(RVS.at[1], RVR.at[d], send_rv.at[d], rv.at[d], xs[d - 1])

    blank = jnp.zeros((8, TOK), F32)
    LT[...] = (
        jnp.concatenate(
            [rg[0], rg[0], rg[1], rg[1], rg[0], rg[2], blank, blank]
            + [sg[0], sg[0], sg[1], sg[1], sg[0], sg[2], blank, blank],
            axis=0,
        )
        .T.astype(BF16)
    )
    mean3 = nn(jnp.concatenate(list(rg) + [blank], axis=0).astype(BF16), H[...])
    sigma3 = nn(jnp.concatenate(list(sg) + [blank], axis=0).astype(BF16), HS[...])
    RY[y, :, 0:HID] = mean3[0:8] + mean3[8:16] + mean3[16:24]
    RY[y, :, HID : 2 * HID] = sigma3[0:8] + sigma3[8:16] + sigma3[16:24]
    R1[...] = jnp.concatenate(
        [am[0], am[1], am[0], am[1], am[2], am[0]] + [gap] * 10, axis=0
    ).astype(BF16)
    R2[...] = jnp.concatenate(
        [gap] * 8 + [sp[0], sp[1], sp[0], sp[1], sp[2], sp[0]] + [gap] * 2, axis=0
    ).astype(BF16)

    step_b(1)
    def rank_terms(k, carry):
        cols = pl.ds(pl.multiple_of(k * CH, CH), CH)
        OWN[:, cols] = nn(LT[...], R1[:, cols]) + IS[:, cols].astype(F32) * nn(LT[...], R2[:, cols])
        return carry

    lax.fori_loop(0, NCH, rank_terms, 0)

    for d in (1, 2, 3):
        landed(RVR.at[d], rv.at[d])
    RVS[2] = RVS[1] + RVR[1] + RVR[2] + RVR[3]
    send(RVS.at[2], RVR.at[4], send_rv.at[4], rv.at[4], other_hi)

    step_d(0)
    step_c(3)
    step_b(2)
    landed(RVR.at[4], rv.at[4])
    ranks = thirds(RVS[2] + RVR[4])
    factor3 = nn(jnp.concatenate(list(ranks) + [blank], axis=0).astype(BF16), OGC[...])
    RY[y, :, 2 * HID :] = factor3[0:8] + factor3[8:16] + factor3[16:24]
    for d in (1, 2, 3):
        send(RY.at[y], RY.at[y], send_ry.at[d - 1], ry.at[d - 1], ys[d - 1])

    step_y(0)
    step_d(1)
    step_c(4)
    step_b(3)
    step_d(2)
    step_y(1)
    step_e(0)
    step_e(1)
    to_self(0, 2)
    step_c(5)
    step_b(4)
    step_d(3)
    step_w(0)
    step_w(1)
    to_partner(0, 2)
    for d in (1, 2, 3):
        landed(RY.at[ring(y, 4 - d)], ry.at[d - 1])
    RZ[z] = ((RY[0] + RY[1]) + RY[2]) + RY[3]
    for d in (1, 2, 3):
        send(RZ.at[z], RZ.at[z], send_rz.at[d - 1], rzz.at[d - 1], zs[d - 1])

    step_c(6)
    step_b(5)
    step_d(4)
    step_e(2)
    step_e(3)
    to_partner(2, 2)
    step_b(6)
    step_d(5)
    to_self(2, 2)
    for d in (1, 2, 3):
        landed(RZ.at[ring(z, 4 - d)], rzz.at[d - 1])
    total = ((RZ[0] + RZ[1]) + RZ[2]) + RZ[3]
    count = 1.0 / math.sqrt(TOK * 16)
    OM[...] = count * total[:, 0:HID]
    OS[...] = count * a_noise[...] * total[:, HID : 2 * HID]
    OF[...] = (count * adapter_scale) * total[:, 2 * HID :]
    put(OM, d_mean)
    put(OS, d_sigma)
    put(OF, d_factor)

    step_d(6)
    finish(0)
    finish(1)
    finish(2)
    finish(3)
    step_e(4)
    step_e(5)
    to_partner(4, 2)
    last = pl.ds(6 * CH, CH)
    PACC[:, 0:CH] = jnp.zeros((TOK, CH), F32)
    part(OGP, PACC, slice(0, CH), last, 0, 6)
    step_e(6)
    part(OGP, PACC, slice(0, CH), last, 6, 8)
    to_pair(6, 0)
    to_self(4, 2)
    finish(4)
    finish(5)
    to_self(6, 1)
    finish(6)

    landed(DW.at[pl.ds(0, 7)], send_dw)
    landed(OGP, send_og)
    landed(RSS, send_rs)
    landed(RVS.at[0], send_rv.at[0])
    for d in (1, 2, 3):
        landed(RVS.at[1], send_rv.at[d])
        landed(RY.at[y], send_ry.at[d - 1])
        landed(RZ.at[z], send_rz.at[d - 1])
    landed(RVS.at[2], send_rv.at[4])
    for copy in out_copies:
        copy.wait()


def hand_over(*refs):
    sources, targets, held, sem = refs[:5], refs[5:10], refs[10:15], refs[15]
    pieces = []
    for n, parts in enumerate((4, 4, 1, 1, 1)):
        step = sources[n].shape[0] // parts
        for m in range(parts):
            rows = pl.ds(m * step, step)
            at = (sources[n].at[rows], held[n].at[rows], targets[n].at[rows])
            pieces.append(
                (
                    pltpu.make_async_copy(at[0], at[1], sem.at[0, len(pieces)]),
                    pltpu.make_async_copy(at[1], at[2], sem.at[1, len(pieces)]),
                )
            )
    for inward, _ in pieces:
        inward.start()
    for inward, outward in pieces:
        inward.wait()
        outward.start()
    for _, outward in pieces:
        outward.wait()


def local(*args):
    anywhere = pl.BlockSpec(memory_space=pl.ANY)
    dma = pltpu.SemaphoreType.DMA
    scratch = [
        pltpu.VMEM((8, HID, WID), BF16),
        pltpu.VMEM((2, TOK, HALF), BF16),
        pltpu.VMEM((2, TOK, HALF), BF16),
        pltpu.VMEM((2, TOK, HALF), BF16),
        pltpu.VMEM((TOK, WID), BF16),
        pltpu.VMEM((TOK, HID), BF16),
        pltpu.VMEM((TOK, HID), BF16),
        pltpu.VMEM((TOK, HID), jnp.int32),
        pltpu.VMEM((TOK, HID), BF16),
        pltpu.VMEM((TOK, HID), BF16),
        pltpu.VMEM((TOK, HID), F32),
        pltpu.VMEM((TOK, HID), F32),
        pltpu.VMEM((TOK, HID), F32),
        pltpu.VMEM((TOK, 2 * CH), F32),
        pltpu.VMEM((NCH, TOK, CH), BF16),
        pltpu.VMEM((NCH, TOK, CH), BF16),
        pltpu.VMEM((128, 4 * HALF), BF16),
        pltpu.VMEM((TOK, 128), BF16),
        pltpu.VMEM((128, HID), BF16),
        pltpu.VMEM((128, HID), BF16),
        pltpu.VMEM((3, 8, TOK), F32),
        pltpu.VMEM((5, 8, TOK), F32),
        pltpu.VMEM((4, 8, RED), F32),
        pltpu.VMEM((4, 8, RED), F32),
        pltpu.VMEM((8, HID), F32),
        pltpu.VMEM((8, HID), F32),
        pltpu.VMEM((8, HID), F32),
        pltpu.VMEM((8, 4 * HALF), F32),
        pltpu.VMEM((8, TOK), jnp.int32),
        pltpu.VMEM((8, HID), F32),
        pltpu.VMEM((8, HID), F32),
        pltpu.VMEM((8, WID), F32),
        dma((14,)),
        dma((2 * NCH + 3,)),
        dma(()),
        dma(()),
        dma(()),
        dma((5,)),
        dma((3,)),
        dma((3,)),
        dma((NCH,)),
        dma((2, NCH)),
        dma((2, NCH)),
        dma((2, 2, NCH)),
        dma((8, 2)),
        dma((NCH,)),
        dma((5,)),
        dma((3,)),
        dma((3,)),
    ]
    shapes = (
        jax.ShapeDtypeStruct((TOK, HID), BF16),
        jax.ShapeDtypeStruct((TOK, HID), BF16),
        jax.ShapeDtypeStruct((8, HID), F32),
        jax.ShapeDtypeStruct((8, HID), F32),
        jax.ShapeDtypeStruct((8, WID), F32),
    )
    results = pl.pallas_call(
        kernel,
        out_shape=shapes,
        in_specs=[anywhere] * 10,
        out_specs=(anywhere,) * 5,
        scratch_shapes=scratch,
        compiler_params=pltpu.CompilerParams(
            collective_id=0, has_side_effects=True, vmem_limit_bytes=58 * 2**20
        ),
        name="ffn_backward",
    )(*args[:9], args[9].T)
    return pl.pallas_call(
        hand_over,
        out_shape=shapes,
        in_specs=[anywhere] * 5,
        out_specs=(anywhere,) * 5,
        scratch_shapes=[pltpu.VMEM(each.shape, each.dtype) for each in shapes] + [dma((2, 11))],
        name="hand_over",
    )(*results)


def solution(mesh):
    placed = (
        P("fsdp", None),
        P("fsdp", "tp"),
        P("fsdp", "tp"),
        P("tp", "fsdp"),
        P(None, "tp"),
        P(None, "tp"),
        P(None, "tp"),
        P(),
        P("fsdp", "tp"),
        P("fsdp", None),
    )
    return jax.shard_map(
        local,
        mesh=mesh,
        in_specs=placed,
        out_specs=(P("fsdp", "tp"), P("fsdp", "tp"), P(None, "tp"), P(None, "tp"), P(None, "tp")),
        check_vma=False,
    )
```

```python
import math

import jax
import jax.numpy as jnp
from jax import lax
from jax.experimental import pallas as pl
from jax.experimental.pallas import tpu as pltpu
from jax.sharding import PartitionSpec as P

MESH = pl.DeviceIdType.MESH
F32 = jnp.float32
BF16 = jnp.bfloat16
adapter_scale = 2.0

TOK = 512
WID = 512
HID = 896
CH = 128
NCH = HID // CH
HALF = 2048
RED = 2 * HID + WID


def nt(left, right):
    return lax.dot_general(left, right, (((1,), (1,)), ((), ())), preferred_element_type=F32)


def nn(left, right):
    return lax.dot_general(left, right, (((1,), (0,)), ((), ())), preferred_element_type=F32)


def thirds(value):
    first = value.astype(BF16).astype(F32)
    rest = value - first
    second = rest.astype(BF16).astype(F32)
    third = (rest - second).astype(BF16).astype(F32)
    return first, second, third


def kernel(
    og,
    gate,
    up,
    dw,
    a_mean_in,
    a_sigma_in,
    a_noise_in,
    factor_in,
    in_signs,
    out_signs_in,
    d_gate,
    d_up,
    d_mean,
    d_sigma,
    d_factor,
    DW,
    OGO,
    OGX,
    OGP,
    OGC,
    G,
    U,
    IS,
    H,
    HS,
    CA,
    CB,
    OWN,
    PACC,
    RSS,
    RSR,
    SF,
    LT,
    R1,
    R2,
    RVS,
    RVR,
    RY,
    RZ,
    a_mean,
    a_sigma,
    a_noise,
    factor,
    out_signs,
    OM,
    OS,
    OF,
    local_sem,
    out_sem,
    send_dw,
    send_og,
    send_rs,
    send_rv,
    send_ry,
    send_rz,
    rz,
    ra,
    rb,
    rc,
    rp,
    rh,
    rr,
    rv,
    ry,
    rzz,
):
    fi = lax.axis_index("fsdp")
    tj = lax.axis_index("tp")
    y, z = lax.rem(fi, 4), lax.div(fi, 4)
    c, x, zh = lax.rem(tj, 2), lax.rem(lax.div(tj, 2), 4), lax.div(tj, 8)
    par, h0 = lax.rem(z, 2), lax.div(z, 2)
    h1 = 1 - h0

    def at(px=x, py=y, pz=z, pzh=zh, pc=c):
        return (pz * 4 + py, (pzh * 4 + px) * 2 + pc)

    def ring(value, step):
        return lax.rem(value + step, 4)

    right, left = at(py=ring(y, 1)), at(py=ring(y, 3))
    pair = at(pz=z + 1 - 2 * par)
    across = at(pz=ring(z, 2))
    sibling = at(pc=1 - c)
    other_hi = at(pzh=1 - zh)
    ys = [at(py=ring(y, d)) for d in (1, 2, 3)]
    zs = [at(pz=ring(z, d)) for d in (1, 2, 3)]
    xs = [at(px=ring(x, d)) for d in (1, 2, 3)]

    barrier = pltpu.get_barrier_semaphore()
    partners = ys + zs + xs + [sibling, other_hi]
    for partner in partners:
        pl.semaphore_signal(barrier, inc=1, device_id=partner, device_id_type=MESH)

    own = h0 * 4 + y
    mirror = h1 * 4 + y

    local = [
        pltpu.make_async_copy(dw, DW.at[own], local_sem.at[0]),
        pltpu.make_async_copy(gate, G, local_sem.at[1]),
        pltpu.make_async_copy(up, U, local_sem.at[2]),
        pltpu.make_async_copy(in_signs, IS, local_sem.at[3]),
        pltpu.make_async_copy(a_mean_in, a_mean, local_sem.at[4]),
        pltpu.make_async_copy(a_sigma_in, a_sigma, local_sem.at[5]),
        pltpu.make_async_copy(a_noise_in, a_noise, local_sem.at[6]),
        pltpu.make_async_copy(out_signs_in, out_signs, local_sem.at[7]),
        pltpu.make_async_copy(factor_in, factor, local_sem.at[8]),
    ]
    early = len(local)
    for h in range(2):
        mine = pl.ds(pl.multiple_of((2 * h + par) * HALF, HALF), HALF)
        rest = pl.ds(pl.multiple_of((2 * h + 1 - par) * HALF, HALF), HALF)
        local.append(pltpu.make_async_copy(og.at[:, mine], OGO.at[h], local_sem.at[9 + 2 * h]))
        local.append(pltpu.make_async_copy(og.at[:, rest], OGX.at[h], local_sem.at[10 + 2 * h]))
    out_cols = pl.ds(pl.multiple_of(tj * WID, WID), WID)
    local.append(pltpu.make_async_copy(og.at[:, out_cols], OGC, local_sem.at[13]))
    for copy in local[1:early]:
        copy.start()

    pl.semaphore_wait(barrier, len(partners))

    def send(src, dst, send_sem, recv_sem, device):
        pltpu.make_async_remote_copy(
            src_ref=src,
            dst_ref=dst,
            send_sem=send_sem,
            recv_sem=recv_sem,
            device_id=device,
            device_id_type=MESH,
        ).start()

    def landed(ref, sem):
        pltpu.make_async_copy(ref, ref, sem).wait()

    def piece(q, h):
        return OGP.at[h, pl.ds(pl.multiple_of(q * 64, 64), 64)]

    q_own = x * 2 + c

    def step_p(h):
        rows = pl.ds(pl.multiple_of(q_own * 64, 64), 64)
        cols = pl.ds(pl.multiple_of((2 * h + 1 - par) * HALF, HALF), HALF)
        send(og.at[rows, cols], piece(q_own, h), send_og, rp.at[q_own, h], pair)

    def step_x(h):
        landed(piece(q_own, h), rp.at[q_own, h])
        for device in (xs[0], xs[2], sibling):
            send(piece(q_own, h), piece(q_own, h), send_og, rp.at[q_own, h], device)

    def half(q, h, side):
        return OGP.at[h, pl.ds(pl.multiple_of(q * 64 + side * 32, 32), 32)]

    def step_y(h):
        for side, d in ((0, 3), (1, 1)):
            q = ring(x, d) * 2 + c
            landed(piece(q, h), rp.at[q, h])
            send(half(q, h, side), half(q, h, side), send_og, rh.at[side, h], xs[(0, 2)[side]])
            send(piece(q, h), piece(q, h), send_og, rp.at[q, h], sibling)

    def step_v(h):
        q = ring(x, 2) * 2 + c
        for side in range(2):
            landed(half(q, h, side), rh.at[side, h])
        send(piece(q, h), piece(q, h), send_og, rp.at[q, h], sibling)

    def step_w(h):
        for px in range(4):
            q = px * 2 + 1 - c
            landed(piece(q, h), rp.at[q, h])

    def rows_of(slot, k, part=None):
        if part is None:
            return DW.at[slot, pl.ds(k * CH, CH)]
        return DW.at[slot, pl.ds(k * CH + part * (CH // 2), CH // 2)]

    def step_z(k):
        send(dw.at[pl.ds(k * CH, CH)], rows_of(own, k), send_dw, rz.at[k], across)

    def step_a(k):
        send(dw.at[pl.ds(k * CH, CH)], rows_of(own, k), send_dw, ra.at[0, k], right)
        send(dw.at[pl.ds(k * CH, CH)], rows_of(own, k), send_dw, ra.at[1, k], left)

    def step_b(k):
        landed(rows_of(mirror, k), rz.at[k])
        send(rows_of(mirror, k), rows_of(mirror, k), send_dw, rb.at[0, k], right)
        send(rows_of(mirror, k), rows_of(mirror, k), send_dw, rb.at[1, k], left)

    def relay(sems, h, group, k):
        slot = h * 4 + ring(y, 3)
        landed(rows_of(slot, k), sems.at[0, k])
        send(rows_of(slot, k, 0), rows_of(slot, k, 0), send_dw, rc.at[0, group, k], right)
        slot = h * 4 + ring(y, 1)
        landed(rows_of(slot, k), sems.at[1, k])
        send(rows_of(slot, k, 1), rows_of(slot, k, 1), send_dw, rc.at[1, group, k], left)

    def step_c(k):
        relay(ra, h0, 0, k)

    def step_d(k):
        relay(rb, h1, 1, k)

    def step_e(k):
        for group, h in ((0, h0), (1, h1)):
            for part in range(2):
                landed(rows_of(h * 4 + ring(y, 2), k, part), rc.at[part, group, k])

    def part(src, acc, acc_cols, rows, low, high):
        def body(m, carry):
            py = ring(y, m + 3)
            kcols = pl.ds(pl.multiple_of(py * WID, WID), WID)
            acc[:, acc_cols] += nt(src[0, :, kcols], DW[py, rows, :]) + nt(src[1, :, kcols], DW[4 + py, rows, :])
            return carry

        lax.fori_loop(low // 2, high // 2, body, 0)

    def to_pair(k, n):
        RSS[k] = PACC[:, n * CH : (n + 1) * CH].astype(BF16)
        send(RSS.at[k], RSR.at[k], send_rs, rr.at[k], pair)

    def to_partner(k, count):
        wide = slice(0, count * CH)
        PACC[:, wide] = jnp.zeros((TOK, count * CH), F32)
        part(OGP, PACC, wide, pl.ds(k * CH, count * CH), 0, 8)
        for n in range(count):
            to_pair(k + n, n)

    def to_self(k, count):
        part(OGO, OWN, slice(k * CH, (k + count) * CH), pl.ds(k * CH, count * CH), 0, 8)

    def part_ry(slot, side):
        return RY.at[slot, :, pl.ds(side * (RED // 2), RED // 2)]

    def relay_ry():
        for side, d in ((0, 3), (1, 1)):
            slot = ring(y, d)
            landed(RY.at[slot], ry.at[side])
            onward = part_ry(slot, side)
            send(onward, onward, send_ry.at[2 + side], ry.at[2 + side], (right, left)[side])

    out_copies = []

    def put(src, dst):
        copy = pltpu.make_async_copy(src, dst, out_sem.at[len(out_copies)])
        copy.start()
        out_copies.append(copy)

    def finish(k):
        cols = slice(k * CH, (k + 1) * CH)
        landed(RSR.at[k], rr.at[k])
        hidden_grad = OWN[:, cols] + RSR[k].astype(F32)
        G[:, cols] = (hidden_grad * CA[:, cols]).astype(BF16)
        U[:, cols] = (hidden_grad * CB[:, cols]).astype(BF16)
        put(G.at[:, pl.ds(k * CH, CH)], d_gate.at[:, pl.ds(k * CH, CH)])
        put(U.at[:, pl.ds(k * CH, CH)], d_up.at[:, pl.ds(k * CH, CH)])

    step_p(0)
    step_p(1)
    for k in range(NCH):
        step_a(k)
    for k in range(NCH):
        step_z(k)
    local[0].start()
    for copy in local[early:]:
        copy.start()

    for n in (1, 2, 3):
        local[n].wait()

    def pre(k, carry):
        cols = pl.ds(pl.multiple_of(k * CH, CH), CH)
        g = G[:, cols].astype(F32)
        u = U[:, cols].astype(F32)
        s = jax.nn.sigmoid(g)
        hidden = (g * s * u).astype(BF16)
        H[:, cols] = hidden
        HS[:, cols] = (hidden.astype(F32) * IS[:, cols].astype(F32)).astype(BF16)
        CA[:, cols] = u * s * (1.0 + g * (1.0 - s))
        CB[:, cols] = g * s
        return carry

    lax.fori_loop(0, NCH, pre, 0)

    for n in range(4, early):
        local[n].wait()
    spread = a_sigma[...] * a_noise[...]
    am = thirds(a_mean[...])
    sp = thirds(spread)
    gap = jnp.zeros((8, HID), F32)
    R1[...] = jnp.concatenate([am[0], am[1], am[2]] + [gap] * 13, axis=0).astype(BF16)
    R2[...] = jnp.concatenate([gap] * 4 + [sp[0], sp[1], sp[2]] + [gap] * 9, axis=0).astype(BF16)
    sign_out = out_signs[...].astype(F32)
    both = (nt(H[...], R1[...]) + nt(HS[...], R2[...])).T
    RVS[0] = (both[0:8] + both[8:16] + both[16:24]) + sign_out * (
        both[32:40] + both[40:48] + both[48:56]
    )
    send(RVS.at[0], RVR.at[0], send_rv.at[0], rv.at[0], sibling)

    step_x(0)
    step_c(0)
    sf = thirds(factor[...])
    SF[...] = jnp.concatenate(
        [sf[0], sf[1], sf[2]] + [jnp.zeros((8, 4 * HALF), F32)] * 13, axis=0
    ).astype(BF16)
    for n in range(early, len(local)):
        local[n].wait()
    local[0].wait()
    LTF = None
    for h in range(2):
        mine = pl.ds(pl.multiple_of((2 * h + par) * HALF, HALF), HALF)
        rest = pl.ds(pl.multiple_of((2 * h + 1 - par) * HALF, HALF), HALF)
        term = nt(OGO[h], SF[:, mine]) + nt(OGX[h], SF[:, rest])
        LTF = term if LTF is None else LTF + term
    turned = LTF.T
    rank_grad = adapter_scale * (turned[0:8] + turned[8:16] + turned[16:24])
    signed = rank_grad * sign_out
    rg = thirds(rank_grad)
    sg = thirds(signed)

    step_x(1)
    step_b(0)
    step_c(1)
    step_c(2)
    landed(RVR.at[0], rv.at[0])
    RVS[1] = RVS[0] + RVR[0]
    for d in (1, 2, 3):
        send(RVS.at[1], RVR.at[d], send_rv.at[d], rv.at[d], xs[d - 1])

    blank = jnp.zeros((8, TOK), F32)
    LT[...] = (
        jnp.concatenate(
            [rg[0], rg[0], rg[1], rg[1], rg[0], rg[2], blank, blank]
            + [sg[0], sg[0], sg[1], sg[1], sg[0], sg[2], blank, blank],
            axis=0,
        )
        .T.astype(BF16)
    )
    mean3 = nn(jnp.concatenate(list(rg) + [blank], axis=0).astype(BF16), H[...])
    sigma3 = nn(jnp.concatenate(list(sg) + [blank], axis=0).astype(BF16), HS[...])
    RY[y, :, 0:HID] = mean3[0:8] + mean3[8:16] + mean3[16:24]
    RY[y, :, HID : 2 * HID] = sigma3[0:8] + sigma3[8:16] + sigma3[16:24]
    R1[...] = jnp.concatenate(
        [am[0], am[1], am[0], am[1], am[2], am[0]] + [gap] * 10, axis=0
    ).astype(BF16)
    R2[...] = jnp.concatenate(
        [gap] * 8 + [sp[0], sp[1], sp[0], sp[1], sp[2], sp[0]] + [gap] * 2, axis=0
    ).astype(BF16)

    step_b(1)
    def rank_terms(k, carry):
        cols = pl.ds(pl.multiple_of(k * CH, CH), CH)
        OWN[:, cols] = nn(LT[...], R1[:, cols]) + IS[:, cols].astype(F32) * nn(LT[...], R2[:, cols])
        return carry

    lax.fori_loop(0, NCH, rank_terms, 0)

    for d in (1, 2, 3):
        landed(RVR.at[d], rv.at[d])
    RVS[2] = RVS[1] + RVR[1] + RVR[2] + RVR[3]
    send(RVS.at[2], RVR.at[4], send_rv.at[4], rv.at[4], other_hi)

    step_d(0)
    step_c(3)
    step_b(2)
    landed(RVR.at[4], rv.at[4])
    ranks = thirds(RVS[2] + RVR[4])
    factor3 = nn(jnp.concatenate(list(ranks) + [blank], axis=0).astype(BF16), OGC[...])
    RY[y, :, 2 * HID :] = factor3[0:8] + factor3[8:16] + factor3[16:24]
    send(RY.at[y], RY.at[y], send_ry.at[0], ry.at[0], right)
    send(RY.at[y], RY.at[y], send_ry.at[1], ry.at[1], left)

    step_y(0)
    step_d(1)
    step_c(4)
    step_b(3)
    step_d(2)
    step_y(1)
    step_e(0)
    step_e(1)
    to_self(0, 2)
    step_c(5)
    step_b(4)
    step_d(3)
    relay_ry()
    step_v(0)
    step_c(6)
    step_b(5)
    step_v(1)
    step_d(4)
    step_w(0)
    step_w(1)
    to_partner(0, 2)
    step_e(2)
    step_e(3)
    to_partner(2, 2)
    for side in range(2):
        landed(part_ry(ring(y, 2), side), ry.at[2 + side])
    RZ[z] = ((RY[0] + RY[1]) + RY[2]) + RY[3]
    for d in (1, 2, 3):
        send(RZ.at[z], RZ.at[z], send_rz.at[d - 1], rzz.at[d - 1], zs[d - 1])

    step_b(6)
    step_d(5)
    to_self(2, 2)
    step_d(6)
    finish(0)
    finish(1)
    finish(2)
    finish(3)
    for d in (1, 2, 3):
        landed(RZ.at[ring(z, 4 - d)], rzz.at[d - 1])
    total = ((RZ[0] + RZ[1]) + RZ[2]) + RZ[3]
    count = 1.0 / math.sqrt(TOK * 16)
    OM[...] = count * total[:, 0:HID]
    OS[...] = count * a_noise[...] * total[:, HID : 2 * HID]
    OF[...] = (count * adapter_scale) * total[:, 2 * HID :]
    put(OM, d_mean)
    put(OS, d_sigma)
    put(OF, d_factor)

    step_e(4)
    step_e(5)
    to_partner(4, 2)
    last = pl.ds(6 * CH, CH)
    PACC[:, 0:CH] = jnp.zeros((TOK, CH), F32)
    part(OGP, PACC, slice(0, CH), last, 0, 6)
    step_e(6)
    part(OGP, PACC, slice(0, CH), last, 6, 8)
    to_pair(6, 0)
    to_self(4, 2)
    finish(4)
    finish(5)
    to_self(6, 1)
    finish(6)

    landed(DW.at[pl.ds(0, 7)], send_dw)
    landed(OGP, send_og)
    landed(RSS, send_rs)
    landed(RVS.at[0], send_rv.at[0])
    for d in (1, 2, 3):
        landed(RVS.at[1], send_rv.at[d])
        landed(RZ.at[z], send_rz.at[d - 1])
    landed(RVS.at[2], send_rv.at[4])
    for side in range(2):
        landed(RY.at[y], send_ry.at[side])
        landed(part_ry(y, side), send_ry.at[2 + side])
    for copy in out_copies:
        copy.wait()


def hand_over(*refs):
    sources, targets, held, sem = refs[:5], refs[5:10], refs[10:15], refs[15]
    pieces = []
    for n, parts in enumerate((4, 4, 1, 1, 1)):
        step = sources[n].shape[0] // parts
        for m in range(parts):
            rows = pl.ds(m * step, step)
            at = (sources[n].at[rows], held[n].at[rows], targets[n].at[rows])
            pieces.append(
                (
                    pltpu.make_async_copy(at[0], at[1], sem.at[0, len(pieces)]),
                    pltpu.make_async_copy(at[1], at[2], sem.at[1, len(pieces)]),
                )
            )
    for inward, _ in pieces:
        inward.start()
    for inward, outward in pieces:
        inward.wait()
        outward.start()
    for _, outward in pieces:
        outward.wait()


def local(*args):
    anywhere = pl.BlockSpec(memory_space=pl.ANY)
    dma = pltpu.SemaphoreType.DMA
    scratch = [
        pltpu.VMEM((8, HID, WID), BF16),
        pltpu.VMEM((2, TOK, HALF), BF16),
        pltpu.VMEM((2, TOK, HALF), BF16),
        pltpu.VMEM((2, TOK, HALF), BF16),
        pltpu.VMEM((TOK, WID), BF16),
        pltpu.VMEM((TOK, HID), BF16),
        pltpu.VMEM((TOK, HID), BF16),
        pltpu.VMEM((TOK, HID), jnp.int32),
        pltpu.VMEM((TOK, HID), BF16),
        pltpu.VMEM((TOK, HID), BF16),
        pltpu.VMEM((TOK, HID), F32),
        pltpu.VMEM((TOK, HID), F32),
        pltpu.VMEM((TOK, HID), F32),
        pltpu.VMEM((TOK, 2 * CH), F32),
        pltpu.VMEM((NCH, TOK, CH), BF16),
        pltpu.VMEM((NCH, TOK, CH), BF16),
        pltpu.VMEM((128, 4 * HALF), BF16),
        pltpu.VMEM((TOK, 128), BF16),
        pltpu.VMEM((128, HID), BF16),
        pltpu.VMEM((128, HID), BF16),
        pltpu.VMEM((3, 8, TOK), F32),
        pltpu.VMEM((5, 8, TOK), F32),
        pltpu.VMEM((4, 8, RED), F32),
        pltpu.VMEM((4, 8, RED), F32),
        pltpu.VMEM((8, HID), F32),
        pltpu.VMEM((8, HID), F32),
        pltpu.VMEM((8, HID), F32),
        pltpu.VMEM((8, 4 * HALF), F32),
        pltpu.VMEM((8, TOK), jnp.int32),
        pltpu.VMEM((8, HID), F32),
        pltpu.VMEM((8, HID), F32),
        pltpu.VMEM((8, WID), F32),
        dma((14,)),
        dma((2 * NCH + 3,)),
        dma(()),
        dma(()),
        dma(()),
        dma((5,)),
        dma((4,)),
        dma((3,)),
        dma((NCH,)),
        dma((2, NCH)),
        dma((2, NCH)),
        dma((2, 2, NCH)),
        dma((8, 2)),
        dma((2, 2)),
        dma((NCH,)),
        dma((5,)),
        dma((4,)),
        dma((3,)),
    ]
    shapes = (
        jax.ShapeDtypeStruct((TOK, HID), BF16),
        jax.ShapeDtypeStruct((TOK, HID), BF16),
        jax.ShapeDtypeStruct((8, HID), F32),
        jax.ShapeDtypeStruct((8, HID), F32),
        jax.ShapeDtypeStruct((8, WID), F32),
    )
    results = pl.pallas_call(
        kernel,
        out_shape=shapes,
        in_specs=[anywhere] * 10,
        out_specs=(anywhere,) * 5,
        scratch_shapes=scratch,
        compiler_params=pltpu.CompilerParams(
            collective_id=0, has_side_effects=True, vmem_limit_bytes=58 * 2**20
        ),
        name="ffn_backward",
    )(*args[:9], args[9].T)
    return pl.pallas_call(
        hand_over,
        out_shape=shapes,
        in_specs=[anywhere] * 5,
        out_specs=(anywhere,) * 5,
        scratch_shapes=[pltpu.VMEM(each.shape, each.dtype) for each in shapes] + [dma((2, 11))],
        name="hand_over",
    )(*results)


def solution(mesh):
    placed = (
        P("fsdp", None),
        P("fsdp", "tp"),
        P("fsdp", "tp"),
        P("tp", "fsdp"),
        P(None, "tp"),
        P(None, "tp"),
        P(None, "tp"),
        P(),
        P("fsdp", "tp"),
        P("fsdp", None),
    )
    return jax.shard_map(
        local,
        mesh=mesh,
        in_specs=placed,
        out_specs=(P("fsdp", "tp"), P("fsdp", "tp"), P(None, "tp"), P(None, "tp"), P(None, "tp")),
        check_vma=False,
    )
```

```python
import math

import jax
import jax.numpy as jnp
from jax import lax
from jax.experimental import pallas as pl
from jax.experimental.pallas import tpu as pltpu
from jax.sharding import PartitionSpec as P

MESH = pl.DeviceIdType.MESH
F32 = jnp.float32
BF16 = jnp.bfloat16
adapter_scale = 2.0

TOK = 512
WID = 512
HID = 896
CH = 128
NCH = HID // CH
HALF = 2048
RED = 2 * HID + WID


def nt(left, right):
    return lax.dot_general(left, right, (((1,), (1,)), ((), ())), preferred_element_type=F32)


def nn(left, right):
    return lax.dot_general(left, right, (((1,), (0,)), ((), ())), preferred_element_type=F32)


def thirds(value):
    first = value.astype(BF16).astype(F32)
    rest = value - first
    second = rest.astype(BF16).astype(F32)
    third = (rest - second).astype(BF16).astype(F32)
    return first, second, third


def kernel(
    og,
    gate,
    up,
    dw,
    a_mean_in,
    a_sigma_in,
    a_noise_in,
    factor_in,
    in_signs,
    out_signs_in,
    d_gate,
    d_up,
    d_mean,
    d_sigma,
    d_factor,
    DW,
    OGO,
    OGX,
    OGP,
    OGC,
    G,
    U,
    IS,
    H,
    HS,
    CA,
    CB,
    OWN,
    PACC,
    RSS,
    RSR,
    SF,
    LT,
    R1,
    R2,
    RVS,
    RVR,
    RY,
    RZ,
    a_mean,
    a_sigma,
    a_noise,
    factor,
    out_signs,
    OM,
    OS,
    OF,
    local_sem,
    out_sem,
    send_dw,
    send_og,
    send_rs,
    send_rv,
    send_ry,
    send_rz,
    rz,
    ra,
    rb,
    rc,
    rp,
    rh,
    rr,
    rv,
    ry,
    rzz,
):
    fi = lax.axis_index("fsdp")
    tj = lax.axis_index("tp")
    y, z = lax.rem(fi, 4), lax.div(fi, 4)
    c, x, zh = lax.rem(tj, 2), lax.rem(lax.div(tj, 2), 4), lax.div(tj, 8)
    par, h0 = lax.rem(z, 2), lax.div(z, 2)
    h1 = 1 - h0

    def at(px=x, py=y, pz=z, pzh=zh, pc=c):
        return (pz * 4 + py, (pzh * 4 + px) * 2 + pc)

    def ring(value, step):
        return lax.rem(value + step, 4)

    right, left = at(py=ring(y, 1)), at(py=ring(y, 3))
    pair = at(pz=z + 1 - 2 * par)
    across = at(pz=ring(z, 2))
    sibling = at(pc=1 - c)
    other_hi = at(pzh=1 - zh)
    ys = [at(py=ring(y, d)) for d in (1, 2, 3)]
    zs = [at(pz=ring(z, d)) for d in (1, 2, 3)]
    xs = [at(px=ring(x, d)) for d in (1, 2, 3)]

    barrier = pltpu.get_barrier_semaphore()
    partners = ys + zs + xs + [sibling, other_hi]
    for partner in partners:
        pl.semaphore_signal(barrier, inc=1, device_id=partner, device_id_type=MESH)

    own = h0 * 4 + y
    mirror = h1 * 4 + y

    local = [
        pltpu.make_async_copy(dw, DW.at[own], local_sem.at[0]),
        pltpu.make_async_copy(gate, G, local_sem.at[1]),
        pltpu.make_async_copy(up, U, local_sem.at[2]),
        pltpu.make_async_copy(in_signs, IS, local_sem.at[3]),
        pltpu.make_async_copy(a_mean_in, a_mean, local_sem.at[4]),
        pltpu.make_async_copy(a_sigma_in, a_sigma, local_sem.at[5]),
        pltpu.make_async_copy(a_noise_in, a_noise, local_sem.at[6]),
        pltpu.make_async_copy(out_signs_in, out_signs, local_sem.at[7]),
        pltpu.make_async_copy(factor_in, factor, local_sem.at[8]),
    ]
    early = len(local)
    for h in range(2):
        mine = pl.ds(pl.multiple_of((2 * h + par) * HALF, HALF), HALF)
        rest = pl.ds(pl.multiple_of((2 * h + 1 - par) * HALF, HALF), HALF)
        local.append(pltpu.make_async_copy(og.at[:, mine], OGO.at[h], local_sem.at[9 + 2 * h]))
        local.append(pltpu.make_async_copy(og.at[:, rest], OGX.at[h], local_sem.at[10 + 2 * h]))
    out_cols = pl.ds(pl.multiple_of(tj * WID, WID), WID)
    local.append(pltpu.make_async_copy(og.at[:, out_cols], OGC, local_sem.at[13]))
    for copy in local[1:early]:
        copy.start()

    pl.semaphore_wait(barrier, len(partners))

    def send(src, dst, send_sem, recv_sem, device):
        pltpu.make_async_remote_copy(
            src_ref=src,
            dst_ref=dst,
            send_sem=send_sem,
            recv_sem=recv_sem,
            device_id=device,
            device_id_type=MESH,
        ).start()

    def landed(ref, sem):
        pltpu.make_async_copy(ref, ref, sem).wait()

    def piece(q, h):
        return OGP.at[h, pl.ds(pl.multiple_of(q * 64, 64), 64)]

    q_own = x * 2 + c

    def step_p(h):
        rows = pl.ds(pl.multiple_of(q_own * 64, 64), 64)
        cols = pl.ds(pl.multiple_of((2 * h + 1 - par) * HALF, HALF), HALF)
        send(og.at[rows, cols], piece(q_own, h), send_og, rp.at[q_own, h], pair)

    def step_x(h):
        landed(piece(q_own, h), rp.at[q_own, h])
        for device in (xs[0], xs[2], sibling):
            send(piece(q_own, h), piece(q_own, h), send_og, rp.at[q_own, h], device)

    def half(q, h, side):
        return OGP.at[h, pl.ds(pl.multiple_of(q * 64 + side * 32, 32), 32)]

    def step_y(h):
        for side, d in ((0, 3), (1, 1)):
            q = ring(x, d) * 2 + c
            landed(piece(q, h), rp.at[q, h])
            send(half(q, h, side), half(q, h, side), send_og, rh.at[side, h], xs[(0, 2)[side]])
            send(piece(q, h), piece(q, h), send_og, rp.at[q, h], sibling)

    def step_v(h):
        q = ring(x, 2) * 2 + c
        for side in range(2):
            landed(half(q, h, side), rh.at[side, h])
        send(piece(q, h), piece(q, h), send_og, rp.at[q, h], sibling)

    def step_w(h):
        for px in range(4):
            q = px * 2 + 1 - c
            landed(piece(q, h), rp.at[q, h])

    def rows_of(slot, k, part=None):
        if part is None:
            return DW.at[slot, pl.ds(k * CH, CH)]
        return DW.at[slot, pl.ds(k * CH + part * (CH // 2), CH // 2)]

    def step_z(k):
        send(dw.at[pl.ds(k * CH, CH)], rows_of(own, k), send_dw, rz.at[k], across)

    def step_a(k):
        send(dw.at[pl.ds(k * CH, CH)], rows_of(own, k), send_dw, ra.at[0, k], right)
        send(dw.at[pl.ds(k * CH, CH)], rows_of(own, k), send_dw, ra.at[1, k], left)

    def step_b(k):
        landed(rows_of(mirror, k), rz.at[k])
        send(rows_of(mirror, k), rows_of(mirror, k), send_dw, rb.at[0, k], right)
        send(rows_of(mirror, k), rows_of(mirror, k), send_dw, rb.at[1, k], left)

    def relay(sems, h, group, k):
        slot = h * 4 + ring(y, 3)
        landed(rows_of(slot, k), sems.at[0, k])
        send(rows_of(slot, k, 0), rows_of(slot, k, 0), send_dw, rc.at[0, group, k], right)
        slot = h * 4 + ring(y, 1)
        landed(rows_of(slot, k), sems.at[1, k])
        send(rows_of(slot, k, 1), rows_of(slot, k, 1), send_dw, rc.at[1, group, k], left)

    def step_c(k):
        relay(ra, h0, 0, k)

    def step_d(k):
        relay(rb, h1, 1, k)

    def step_e(k):
        for group, h in ((0, h0), (1, h1)):
            for part in range(2):
                landed(rows_of(h * 4 + ring(y, 2), k, part), rc.at[part, group, k])

    def part(src, acc, acc_cols, rows, low, high):
        def body(m, carry):
            py = ring(y, m + 3)
            kcols = pl.ds(pl.multiple_of(py * WID, WID), WID)
            acc[:, acc_cols] += nt(src[0, :, kcols], DW[py, rows, :]) + nt(src[1, :, kcols], DW[4 + py, rows, :])
            return carry

        lax.fori_loop(low // 2, high // 2, body, 0)

    def to_pair(k, n):
        RSS[k] = PACC[:, n * CH : (n + 1) * CH].astype(BF16)
        send(RSS.at[k], RSR.at[k], send_rs, rr.at[k], pair)

    def to_partner(k, count):
        wide = slice(0, count * CH)
        PACC[:, wide] = jnp.zeros((TOK, count * CH), F32)
        part(OGP, PACC, wide, pl.ds(k * CH, count * CH), 0, 8)
        for n in range(count):
            to_pair(k + n, n)

    def to_self(k, count):
        part(OGO, OWN, slice(k * CH, (k + count) * CH), pl.ds(k * CH, count * CH), 0, 8)

    def part_ry(slot, side):
        return RY.at[slot, :, pl.ds(side * (RED // 2), RED // 2)]

    def relay_ry():
        for side, d in ((0, 3), (1, 1)):
            slot = ring(y, d)
            landed(RY.at[slot], ry.at[side])
            onward = part_ry(slot, side)
            send(onward, onward, send_ry.at[2 + side], ry.at[2 + side], (right, left)[side])

    out_copies = []

    def put(src, dst):
        copy = pltpu.make_async_copy(src, dst, out_sem.at[len(out_copies)])
        copy.start()
        out_copies.append(copy)

    def finish(k):
        cols = slice(k * CH, (k + 1) * CH)
        landed(RSR.at[k], rr.at[k])
        hidden_grad = OWN[:, cols] + RSR[k].astype(F32)
        G[:, cols] = (hidden_grad * CA[:, cols]).astype(BF16)
        U[:, cols] = (hidden_grad * CB[:, cols]).astype(BF16)
        put(G.at[:, pl.ds(k * CH, CH)], d_gate.at[:, pl.ds(k * CH, CH)])
        put(U.at[:, pl.ds(k * CH, CH)], d_up.at[:, pl.ds(k * CH, CH)])

    step_p(0)
    step_p(1)
    for k in range(NCH):
        step_a(k)
    for k in range(NCH):
        step_z(k)
    local[0].start()
    for copy in local[early:]:
        copy.start()

    for n in (1, 2, 3):
        local[n].wait()

    def pre(k, carry):
        cols = pl.ds(pl.multiple_of(k * CH, CH), CH)
        g = G[:, cols].astype(F32)
        u = U[:, cols].astype(F32)
        s = jax.nn.sigmoid(g)
        hidden = (g * s * u).astype(BF16)
        H[:, cols] = hidden
        HS[:, cols] = (hidden.astype(F32) * IS[:, cols].astype(F32)).astype(BF16)
        CA[:, cols] = u * s * (1.0 + g * (1.0 - s))
        CB[:, cols] = g * s
        return carry

    lax.fori_loop(0, NCH, pre, 0)

    for n in range(4, early):
        local[n].wait()
    spread = a_sigma[...] * a_noise[...]
    am = thirds(a_mean[...])
    sp = thirds(spread)
    gap = jnp.zeros((8, HID), F32)
    R1[...] = jnp.concatenate([am[0], am[1], am[2]] + [gap] * 13, axis=0).astype(BF16)
    R2[...] = jnp.concatenate([gap] * 4 + [sp[0], sp[1], sp[2]] + [gap] * 9, axis=0).astype(BF16)
    sign_out = out_signs[...].astype(F32)
    both = (nt(H[...], R1[...]) + nt(HS[...], R2[...])).T
    RVS[0] = (both[0:8] + both[8:16] + both[16:24]) + sign_out * (
        both[32:40] + both[40:48] + both[48:56]
    )
    send(RVS.at[0], RVR.at[0], send_rv.at[0], rv.at[0], sibling)

    step_x(0)
    step_c(0)
    sf = thirds(factor[...])
    SF[...] = jnp.concatenate(
        [sf[0], sf[1], sf[2]] + [jnp.zeros((8, 4 * HALF), F32)] * 13, axis=0
    ).astype(BF16)
    for n in range(early, len(local)):
        local[n].wait()
    local[0].wait()
    LTF = None
    for h in range(2):
        mine = pl.ds(pl.multiple_of((2 * h + par) * HALF, HALF), HALF)
        rest = pl.ds(pl.multiple_of((2 * h + 1 - par) * HALF, HALF), HALF)
        term = nt(OGO[h], SF[:, mine]) + nt(OGX[h], SF[:, rest])
        LTF = term if LTF is None else LTF + term
    turned = LTF.T
    rank_grad = adapter_scale * (turned[0:8] + turned[8:16] + turned[16:24])
    signed = rank_grad * sign_out
    rg = thirds(rank_grad)
    sg = thirds(signed)

    step_x(1)
    step_b(0)
    step_c(1)
    step_c(2)
    landed(RVR.at[0], rv.at[0])
    RVS[1] = RVS[0] + RVR[0]
    for d in (1, 2, 3):
        send(RVS.at[1], RVR.at[d], send_rv.at[d], rv.at[d], xs[d - 1])

    blank = jnp.zeros((8, TOK), F32)
    LT[...] = (
        jnp.concatenate(
            [rg[0], rg[0], rg[1], rg[1], rg[0], rg[2], blank, blank]
            + [sg[0], sg[0], sg[1], sg[1], sg[0], sg[2], blank, blank],
            axis=0,
        )
        .T.astype(BF16)
    )
    mean3 = nn(jnp.concatenate(list(rg) + [blank], axis=0).astype(BF16), H[...])
    sigma3 = nn(jnp.concatenate(list(sg) + [blank], axis=0).astype(BF16), HS[...])
    RY[y, :, 0:HID] = mean3[0:8] + mean3[8:16] + mean3[16:24]
    RY[y, :, HID : 2 * HID] = sigma3[0:8] + sigma3[8:16] + sigma3[16:24]
    R1[...] = jnp.concatenate(
        [am[0], am[1], am[0], am[1], am[2], am[0]] + [gap] * 10, axis=0
    ).astype(BF16)
    R2[...] = jnp.concatenate(
        [gap] * 8 + [sp[0], sp[1], sp[0], sp[1], sp[2], sp[0]] + [gap] * 2, axis=0
    ).astype(BF16)

    step_b(1)
    def rank_terms(k, carry):
        cols = pl.ds(pl.multiple_of(k * CH, CH), CH)
        OWN[:, cols] = nn(LT[...], R1[:, cols]) + IS[:, cols].astype(F32) * nn(LT[...], R2[:, cols])
        return carry

    lax.fori_loop(0, NCH, rank_terms, 0)

    for d in (1, 2, 3):
        landed(RVR.at[d], rv.at[d])
    RVS[2] = RVS[1] + RVR[1] + RVR[2] + RVR[3]
    send(RVS.at[2], RVR.at[4], send_rv.at[4], rv.at[4], other_hi)

    step_d(0)
    step_c(3)
    step_b(2)
    landed(RVR.at[4], rv.at[4])
    ranks = thirds(RVS[2] + RVR[4])
    factor3 = nn(jnp.concatenate(list(ranks) + [blank], axis=0).astype(BF16), OGC[...])
    RY[y, :, 2 * HID :] = factor3[0:8] + factor3[8:16] + factor3[16:24]
    send(RY.at[y], RY.at[y], send_ry.at[0], ry.at[0], right)
    send(RY.at[y], RY.at[y], send_ry.at[1], ry.at[1], left)

    step_y(0)
    step_d(1)
    step_c(4)
    step_b(3)
    step_d(2)
    step_y(1)
    step_e(0)
    step_e(1)
    to_self(0, 2)
    step_c(5)
    step_b(4)
    step_d(3)
    relay_ry()
    step_v(0)
    step_c(6)
    step_b(5)
    step_v(1)
    step_d(4)
    step_w(0)
    step_w(1)
    to_partner(0, 2)
    step_e(2)
    step_e(3)
    to_partner(2, 2)
    for side in range(2):
        landed(part_ry(ring(y, 2), side), ry.at[2 + side])
    RZ[z] = ((RY[0] + RY[1]) + RY[2]) + RY[3]
    for d in (1, 2, 3):
        send(RZ.at[z], RZ.at[z], send_rz.at[d - 1], rzz.at[d - 1], zs[d - 1])

    step_b(6)
    step_d(5)
    to_self(2, 2)
    step_d(6)
    finish(0)
    finish(1)
    for d in (1, 2, 3):
        landed(RZ.at[ring(z, 4 - d)], rzz.at[d - 1])
    total = ((RZ[0] + RZ[1]) + RZ[2]) + RZ[3]
    count = 1.0 / math.sqrt(TOK * 16)
    OM[...] = count * total[:, 0:HID]
    OS[...] = count * a_noise[...] * total[:, HID : 2 * HID]
    OF[...] = (count * adapter_scale) * total[:, 2 * HID :]
    put(OM, d_mean)
    put(OS, d_sigma)
    put(OF, d_factor)

    step_e(4)
    step_e(5)
    to_partner(4, 2)
    finish(2)
    finish(3)
    last = pl.ds(6 * CH, CH)
    PACC[:, 0:CH] = jnp.zeros((TOK, CH), F32)
    part(OGP, PACC, slice(0, CH), last, 0, 6)
    step_e(6)
    part(OGP, PACC, slice(0, CH), last, 6, 8)
    to_pair(6, 0)
    to_self(4, 2)
    finish(4)
    finish(5)
    to_self(6, 1)
    finish(6)

    landed(DW.at[pl.ds(0, 7)], send_dw)
    landed(OGP, send_og)
    landed(RSS, send_rs)
    landed(RVS.at[0], send_rv.at[0])
    for d in (1, 2, 3):
        landed(RVS.at[1], send_rv.at[d])
        landed(RZ.at[z], send_rz.at[d - 1])
    landed(RVS.at[2], send_rv.at[4])
    for side in range(2):
        landed(RY.at[y], send_ry.at[side])
        landed(part_ry(y, side), send_ry.at[2 + side])
    for copy in out_copies:
        copy.wait()


def hand_over(*refs):
    sources, targets, held, sem = refs[:5], refs[5:10], refs[10:15], refs[15]
    pieces = []
    for n, parts in enumerate((4, 4, 1, 1, 1)):
        step = sources[n].shape[0] // parts
        for m in range(parts):
            rows = pl.ds(m * step, step)
            at = (sources[n].at[rows], held[n].at[rows], targets[n].at[rows])
            pieces.append(
                (
                    pltpu.make_async_copy(at[0], at[1], sem.at[0, len(pieces)]),
                    pltpu.make_async_copy(at[1], at[2], sem.at[1, len(pieces)]),
                )
            )
    for inward, _ in pieces:
        inward.start()
    for inward, outward in pieces:
        inward.wait()
        outward.start()
    for _, outward in pieces:
        outward.wait()


def local(*args):
    anywhere = pl.BlockSpec(memory_space=pl.ANY)
    dma = pltpu.SemaphoreType.DMA
    scratch = [
        pltpu.VMEM((8, HID, WID), BF16),
        pltpu.VMEM((2, TOK, HALF), BF16),
        pltpu.VMEM((2, TOK, HALF), BF16),
        pltpu.VMEM((2, TOK, HALF), BF16),
        pltpu.VMEM((TOK, WID), BF16),
        pltpu.VMEM((TOK, HID), BF16),
        pltpu.VMEM((TOK, HID), BF16),
        pltpu.VMEM((TOK, HID), jnp.int32),
        pltpu.VMEM((TOK, HID), BF16),
        pltpu.VMEM((TOK, HID), BF16),
        pltpu.VMEM((TOK, HID), F32),
        pltpu.VMEM((TOK, HID), F32),
        pltpu.VMEM((TOK, HID), F32),
        pltpu.VMEM((TOK, 2 * CH), F32),
        pltpu.VMEM((NCH, TOK, CH), BF16),
        pltpu.VMEM((NCH, TOK, CH), BF16),
        pltpu.VMEM((128, 4 * HALF), BF16),
        pltpu.VMEM((TOK, 128), BF16),
        pltpu.VMEM((128, HID), BF16),
        pltpu.VMEM((128, HID), BF16),
        pltpu.VMEM((3, 8, TOK), F32),
        pltpu.VMEM((5, 8, TOK), F32),
        pltpu.VMEM((4, 8, RED), F32),
        pltpu.VMEM((4, 8, RED), F32),
        pltpu.VMEM((8, HID), F32),
        pltpu.VMEM((8, HID), F32),
        pltpu.VMEM((8, HID), F32),
        pltpu.VMEM((8, 4 * HALF), F32),
        pltpu.VMEM((8, TOK), jnp.int32),
        pltpu.VMEM((8, HID), F32),
        pltpu.VMEM((8, HID), F32),
        pltpu.VMEM((8, WID), F32),
        dma((14,)),
        dma((2 * NCH + 3,)),
        dma(()),
        dma(()),
        dma(()),
        dma((5,)),
        dma((4,)),
        dma((3,)),
        dma((NCH,)),
        dma((2, NCH)),
        dma((2, NCH)),
        dma((2, 2, NCH)),
        dma((8, 2)),
        dma((2, 2)),
        dma((NCH,)),
        dma((5,)),
        dma((4,)),
        dma((3,)),
    ]
    shapes = (
        jax.ShapeDtypeStruct((TOK, HID), BF16),
        jax.ShapeDtypeStruct((TOK, HID), BF16),
        jax.ShapeDtypeStruct((8, HID), F32),
        jax.ShapeDtypeStruct((8, HID), F32),
        jax.ShapeDtypeStruct((8, WID), F32),
    )
    results = pl.pallas_call(
        kernel,
        out_shape=shapes,
        in_specs=[anywhere] * 10,
        out_specs=(anywhere,) * 5,
        scratch_shapes=scratch,
        compiler_params=pltpu.CompilerParams(
            collective_id=0, has_side_effects=True, vmem_limit_bytes=58 * 2**20
        ),
        name="ffn_backward",
    )(*args[:9], args[9].T)
    return pl.pallas_call(
        hand_over,
        out_shape=shapes,
        in_specs=[anywhere] * 5,
        out_specs=(anywhere,) * 5,
        scratch_shapes=[pltpu.VMEM(each.shape, each.dtype) for each in shapes] + [dma((2, 11))],
        name="hand_over",
    )(*results)


def solution(mesh):
    placed = (
        P("fsdp", None),
        P("fsdp", "tp"),
        P("fsdp", "tp"),
        P("tp", "fsdp"),
        P(None, "tp"),
        P(None, "tp"),
        P(None, "tp"),
        P(),
        P("fsdp", "tp"),
        P("fsdp", None),
    )
    return jax.shard_map(
        local,
        mesh=mesh,
        in_specs=placed,
        out_specs=(P("fsdp", "tp"), P("fsdp", "tp"), P(None, "tp"), P(None, "tp"), P(None, "tp")),
        check_vma=False,
    )
```
